256 devices in a mesh: pipe: 32 (over z, y), tensor: 8 (over x, core).
Axes of the slice: x: 4, y: 4, z: 8, core: 2. Of those that a mesh axis runs over, the one named last changes fastest.
Arguments:
- gate_pre: bfloat16 [256, 53248], P(None, 'pipe'), may hold values from -8 to 8
- up_pre: bfloat16 [256, 53248], P(None, 'pipe'), may hold values from -8 to 8
- down_codes: bfloat16 [53248, 16384], P('pipe', 'tensor'), may hold values from -6 to 6, as said below
- down_scales: bfloat16 [3328, 16384], P('pipe', 'tensor'), may hold values from 0.5 to 2
- weight_scale: float32 [1], replicated, may hold values from 0.0017334381 to 0.0043335953
- residual: bfloat16 [256, 16384], P('pipe', 'tensor'), may hold values from -17 to 17
- norm_gain: bfloat16 [16384], P('tensor'), may hold values from 0.5 to 1.5
Outputs:
- payload: bfloat16 [256, 53248], P(None, 'pipe')
- block_scales: float32 [256, 3328], P(None, 'pipe')
- new_residual: bfloat16 [256, 16384], P('pipe', 'tensor')
- normed: bfloat16 [256, 16384], P('pipe', 'tensor')
The draws below stay inside these ranges and needn't reach their ends.
Inputs may be any that keep to these rules, and one draw needn't show every extreme that they name: Every entry of down_codes is 0 or plus or minus 0.5, 1, 1.5, 2, 3, 4 or 6.
All inputs are finite; a program needn't handle non-finite values. Where the reference program divides by a largest or mean magnitude, that divisor is 1e-20 or more.
Results may differ from the reference program's by a relative error of at most 0.0085.
Values sent between devices are 32-bit elements; how exact they have to be, the bound alone decides.
No kernel may reach another device: no remote copies, remote signals or barrier semaphores. Data moves between devices by JAX's collectives and lax.ppermute only.
A program may use at most 128 MiB of HBM per device.

```python
import math
import jax
import jax.numpy as jnp
from jax import lax

D = 16384
FF = 53248
ROWS = 256
N_PIPE = 32


def scaled_field(key, row_count, col_count):
    keys = jax.random.split(key, 3)
    base = jnp.clip(jax.random.normal(keys[0], (row_count, col_count), jnp.float32), -4.0, 4.0)
    row_scale = jnp.exp(jax.random.uniform(keys[1], (row_count, 1), jnp.float32, -1.15, 0.0))
    col_scale = jnp.exp(jax.random.uniform(keys[2], (1, col_count), jnp.float32, -0.69, 0.69))
    return base * row_scale * col_scale


def draw_gate_pre(key, part):
    key = jax.random.fold_in(key, 1)
    return scaled_field(key, ROWS, FF).astype(jnp.bfloat16)


def draw_up_pre(key, part):
    key = jax.random.fold_in(key, 2)
    field = scaled_field(key, ROWS, FF)
    quiet_keys = jax.random.split(jax.random.fold_in(key, 7), 2)
    ranking = jax.random.permutation(quiet_keys[0], ROWS)
    quiet_rows = ranking < max(2, ROWS // 16)
    depth = jax.random.uniform(quiet_keys[1], (ROWS,), jnp.float32, -6.0, -2.5)
    factor = jnp.where(quiet_rows, jnp.exp(depth), 1.0)
    return (field * factor[:, None]).astype(jnp.bfloat16)


def draw_down_codes(key, part):
    key = jax.random.fold_in(key, 3)
    grid_values = jnp.array([0.0, 0.5, 1.0, 1.5, 2.0, 3.0, 4.0, 6.0], jnp.float32)
    picks = jax.random.randint(key, (FF, D), 0, 16)
    magnitude = grid_values[picks % 8]
    return (magnitude * (1 - 2 * (picks // 8)).astype(jnp.float32)).astype(jnp.bfloat16)


def draw_residual(key, part):
    key = jax.random.fold_in(key, 4)
    keys = jax.random.split(key, 2)
    columns = jnp.arange(D, dtype=jnp.float32) / D
    rising = jnp.exp(columns * 1.0986) * jnp.exp(jax.random.uniform(keys[1], (1, D), jnp.float32, -0.35, 0.33))
    base = jnp.clip(jax.random.normal(keys[0], (ROWS, D), jnp.float32), -4.0, 4.0)
    return (base * rising).astype(jnp.bfloat16)


def steps_of(rng, extent, cuts, smallest, largest):
    gain = 1.0
    for position, blocks in cuts:
        heights = jax.random.uniform(jax.random.fold_in(jax.random.fold_in(rng, 6), position), (blocks,), jnp.float32, smallest / len(cuts), largest / len(cuts))
        gain = gain * jnp.repeat(jnp.exp(heights), extent[position] // blocks).reshape((-1,) + (1,) * (len(extent) - 1 - position))
    return gain


def setup_inputs(seed: int = 0) -> dict:
    key_list = jax.random.split(jax.random.key(seed), 8)
    gate_pre = draw_gate_pre(jax.random.fold_in(key_list[7], 71), 0)
    up_pre = draw_up_pre(jax.random.fold_in(key_list[7], 71), 0)
    down_codes = draw_down_codes(jax.random.fold_in(key_list[7], 71), 0)
    down_scales = jnp.clip(jnp.exp(math.log(2.0) - 1.3862944 * jax.random.uniform(key_list[3], (FF // 16, D), jnp.float32) ** steps_of(key_list[3], (FF // 16, D), ((0, 32), (1, 8)), -0.2, 0.2)), 0.5, 2.0).astype(jnp.bfloat16)
    weight_scale = jnp.clip(jnp.exp(jax.random.uniform(key_list[4], (1,), jnp.float32, math.log(0.0017334381), math.log(0.0043335953))), 0.0017334381, 0.0043335953)
    residual = draw_residual(jax.random.fold_in(key_list[7], 71), 0)
    norm_gain = jnp.clip(1.0 + 0.1 * jax.random.normal(key_list[6], (D,), jnp.float32), 0.5, 1.5).astype(jnp.bfloat16)
    return dict(gate_pre=gate_pre, up_pre=up_pre, down_codes=down_codes, down_scales=down_scales, weight_scale=weight_scale, residual=residual, norm_gain=norm_gain)


def sylvester_signs(order_size):
    indices = jnp.arange(order_size, dtype=jnp.int32)
    intersection = jnp.bitwise_and(indices[:, None], indices[None, :])
    parity = jnp.zeros((order_size, order_size), jnp.int32)
    for level in range(order_size.bit_length() - 1):
        parity = parity + jnp.bitwise_and(jnp.right_shift(intersection, level), 1)
    return (1 - 2 * (parity % 2)).astype(jnp.float32)

def reference(gate_pre, up_pre, down_codes, down_scales, weight_scale, residual, norm_gain):
    groups = FF // (128 * N_PIPE)
    hidden = (jax.nn.silu(gate_pre.astype(jnp.float32)) * up_pre.astype(jnp.float32)).astype(jnp.bfloat16)
    hidden_cube = hidden.astype(jnp.float32).reshape(ROWS, N_PIPE, groups, 128)
    inner = jnp.einsum('rpcj,jk->rpck', hidden_cube, sylvester_signs(128), precision=lax.Precision.HIGHEST)
    mixed = jnp.einsum('pq,rqck->rpck', sylvester_signs(N_PIPE), inner, precision=lax.Precision.HIGHEST)
    rotated = mixed * (1.0 / math.sqrt(128 * N_PIPE))
    peak_value = jnp.max(jnp.abs(rotated))
    blocks = rotated.reshape(ROWS, N_PIPE, groups, 8, 16)
    block_bound = jnp.maximum(lax.optimization_barrier(jnp.max(jnp.abs(blocks), axis=4)), peak_value / 64.0)
    block_scales = (448.0 * block_bound / peak_value).reshape(ROWS, FF // 16)
    payload = (6.0 * blocks / block_bound[..., None]).astype(jnp.bfloat16)
    dequant = (payload.astype(jnp.float32) * block_bound[..., None] / 6.0).astype(jnp.bfloat16).reshape(ROWS, FF)
    block_rows = 128 * N_PIPE

    def accumulate(carry, index):
        row_start = index * block_rows
        codes_part = lax.dynamic_slice_in_dim(down_codes, row_start, block_rows, 0)
        scales_part = lax.dynamic_slice_in_dim(down_scales, index * (block_rows // 16), block_rows // 16, 0)
        acts = lax.dynamic_slice_in_dim(dequant, row_start, block_rows, 1)
        weight = (codes_part.reshape(block_rows // 16, 16, D).astype(jnp.float32) * scales_part[:, None, :].astype(jnp.float32) * weight_scale[0]).reshape(block_rows, D).astype(jnp.bfloat16)
        return (carry + jnp.dot(acts, weight, preferred_element_type=jnp.float32), None)
    down_sum, unused = lax.scan(accumulate, jnp.zeros((ROWS, D), jnp.float32), jnp.arange(FF // block_rows, dtype=jnp.int32))
    summed = residual.astype(jnp.float32) + down_sum
    mean_square = lax.optimization_barrier(jnp.sum(summed * summed, axis=1)) / D
    normed = (summed * lax.rsqrt(mean_square + 1e-05)[:, None] * norm_gain.astype(jnp.float32)).astype(jnp.bfloat16)
    return (payload.reshape(ROWS, FF), block_scales, summed.astype(jnp.bfloat16), normed)
```

```python
import functools

import jax
import jax.numpy as jnp
import numpy as np
from jax import lax
from jax.experimental import pallas as pl
from jax.experimental.pallas import tpu as pltpu
from jax.sharding import Mesh
from jax.sharding import PartitionSpec as P

NZ, NY, NX, NC = 8, 4, 4, 2
N_PIPE, N_TENSOR = NZ * NY, NX * NC
ROWS, GROUPS, INNER = 256, 13, 128
WIDTH = GROUPS * INNER
COLS = 2048
WIDE = COLS + 128
SLAB = ROWS // N_TENSOR
OWN = ROWS // N_PIPE
SIZES = {"z": NZ, "y": NY, "x": NX, "c": NC}
VMEM = pl.BlockSpec(memory_space=pltpu.VMEM)
PARAMS = pltpu.CompilerParams(vmem_limit_bytes=48 * 1024 * 1024)


def signs(order):
    i = np.arange(order)
    parity = np.zeros((order, order), np.int64)
    for level in range(order.bit_length()):
        parity += ((i[:, None] & i[None, :]) >> level) & 1
    return (1 - 2 * (parity % 2)).astype(np.float32)


def moved(block, axis, step):
    count = SIZES[axis]
    return lax.ppermute(block, axis, [(i, (i + step) % count) for i in range(count)])


def inner_kernel(place, gate, up, had, out):
    g = gate[...].astype(jnp.float32)
    hidden = (g / (1.0 + jnp.exp(-g)) * up[...].astype(jnp.float32)).astype(jnp.bfloat16)
    for c in range(GROUPS):
        cols = slice(c * INNER, (c + 1) * INNER)
        out[:, cols] = jnp.dot(hidden[:, cols], had[...], preferred_element_type=jnp.float32)


def inner_transform(gate_pre, up_pre, place):
    had = jnp.asarray(signs(INNER) / 64.0, jnp.bfloat16)
    return pl.pallas_call(
        inner_kernel,
        grid_spec=pltpu.PrefetchScalarGridSpec(
            num_scalar_prefetch=1,
            grid=(1,),
            in_specs=[
                pl.BlockSpec((SLAB, WIDTH), lambda i, place: (place[0], 0)),
                pl.BlockSpec((SLAB, WIDTH), lambda i, place: (place[0], 0)),
                pl.BlockSpec((INNER, INNER), lambda i, place: (0, 0)),
            ],
            out_specs=pl.BlockSpec((SLAB, WIDTH), lambda i, place: (0, 0)),
        ),
        out_shape=jax.ShapeDtypeStruct((SLAB, WIDTH), jnp.float32),
        compiler_params=PARAMS,
        name="inner_transform",
    )(place, gate_pre, up_pre, had)


def outer_kernel(block, had, out):
    out[...] = jnp.dot(
        had[...], block[...], preferred_element_type=jnp.float32, precision=lax.Precision.HIGHEST
    )


def outer_transform(block):
    had = jnp.asarray(signs(N_PIPE), jnp.float32)
    return pl.pallas_call(
        outer_kernel,
        in_specs=[VMEM, VMEM],
        out_specs=VMEM,
        out_shape=jax.ShapeDtypeStruct((N_PIPE, WIDTH), jnp.float32),
        compiler_params=PARAMS,
        name="outer_transform",
    )(block, had)


BN = 256


def product_kernel(place, *refs):
    slabs, (codes, scales), outs, (rows32, rows16, peak) = refs[:8], refs[8:10], refs[10:15], refs[15:]
    step = pl.program_id(0)

    @pl.when(step == 0)
    def _():
        my_z, my_y, my_x, my_c = place[0], place[1], place[2], place[3]
        top = jnp.zeros((8, WIDTH), jnp.float32)
        for j, slab in enumerate(slabs):
            dx, dc = j // NC, j % NC
            z = lax.rem(my_x + NX - dx, NX) * NC + lax.rem(my_c + dc, NC)
            z_step = lax.rem(z - my_z + NZ, NZ)
            for y in range(NY):
                y_step = lax.rem(y - my_y + NY, NY)
                piece = slab[y * OWN : (y + 1) * OWN, :]
                top = jnp.maximum(top, jnp.abs(piece))
                at = pl.multiple_of(y_step * (NZ * OWN) + z_step * OWN, OWN)
                rows32[pl.ds(at, OWN), :] = piece
        rows16[...] = rows32[...].astype(jnp.bfloat16)
        peak[...] = jnp.full((8, 128), jnp.max(top), jnp.float32)
        for out in outs:
            for k in range(out.shape[0] // 8):
                out[k * 8 : (k + 1) * 8, COLS:] = peak[...]

    s = scales[...]
    w = codes[...] * jnp.broadcast_to(s[:, None, :], (WIDTH // 16, 16, BN)).reshape(WIDTH, BN)
    total = jnp.dot(rows16[...], w, preferred_element_type=jnp.float32)
    cols = pl.ds(pl.multiple_of(step * BN, BN), BN)
    at = 0
    for out in outs:
        out[:, cols] = total[at : at + out.shape[0], :]
        at += out.shape[0]


def product(slabs, codes, scales, place):
    sizes = [64, 64, 32, 32, 64]
    full = lambda shape: pl.BlockSpec(shape, lambda i, place: (0, 0))
    return pl.pallas_call(
        product_kernel,
        grid_spec=pltpu.PrefetchScalarGridSpec(
            num_scalar_prefetch=1,
            grid=(COLS // BN,),
            in_specs=[full((SLAB, WIDTH))] * 8
            + [
                pl.BlockSpec((WIDTH, BN), lambda i, place: (0, i)),
                pl.BlockSpec((WIDTH // 16, BN), lambda i, place: (0, i)),
            ],
            out_specs=[full((n, WIDE)) for n in sizes],
            scratch_shapes=[
                pltpu.VMEM((ROWS, WIDTH), jnp.float32),
                pltpu.VMEM((ROWS, WIDTH), jnp.bfloat16),
                pltpu.VMEM((8, 128), jnp.float32),
            ],
        ),
        out_shape=[jax.ShapeDtypeStruct((n, WIDE), jnp.float32) for n in sizes],
        compiler_params=PARAMS,
        name="product",
    )(place, *slabs, codes, scales)


def relay_kernel(a, first, b, second, out_a, out_b):
    out_a[...] = a[...]
    out_b[...] = b[...]
    out_a[:32, :COLS] += first[:, :COLS]
    out_b[32:, :COLS] += second[:, :COLS]
    other = jnp.maximum(first[:, COLS:], second[:, COLS:])
    out_a[:32, COLS:] = jnp.maximum(a[:32, COLS:], other)
    out_b[:32, COLS:] = jnp.maximum(b[:32, COLS:], other)


def relay(a, first, b, second):
    shape = jax.ShapeDtypeStruct((64, WIDE), jnp.float32)
    return pl.pallas_call(
        relay_kernel,
        in_specs=[VMEM] * 4,
        out_specs=[VMEM] * 2,
        out_shape=[shape] * 2,
        compiler_params=PARAMS,
        name="relay",
    )(a, first, b, second)


def y_sum_kernel(a, b, c, *outs):
    top = jnp.maximum(jnp.maximum(a[:8, COLS:], b[:8, COLS:]), c[:8, COLS:])
    for k, out in enumerate(outs):
        r = slice(k * OWN, (k + 1) * OWN)
        out[:, :COLS] = a[r, :COLS] + b[r, :COLS] + c[r, :COLS]
        out[:, COLS:] = top


def y_sum(a, b, c):
    return pl.pallas_call(
        y_sum_kernel,
        in_specs=[VMEM] * 3,
        out_specs=[VMEM] * NZ,
        out_shape=[jax.ShapeDtypeStruct((OWN, WIDE), jnp.float32)] * NZ,
        compiler_params=PARAMS,
        name="y_sum",
    )(a, b, c)


def z_sum_kernel(*refs):
    parts, residual, scale, summed, rounded, squares, top = refs[:NZ], *refs[NZ:]
    total = parts[0][:, :COLS]
    peak = parts[0][:, COLS:]
    for part in parts[1:]:
        total += part[:, :COLS]
        peak = jnp.maximum(peak, part[:, COLS:])
    total = residual[...].astype(jnp.float32) + total * scale[0]
    summed[...] = total
    rounded[...] = total.astype(jnp.bfloat16)
    squares[...] = jnp.broadcast_to(jnp.sum(total * total, axis=1, keepdims=True), (OWN, 128))
    top[...] = peak


def z_sum(parts, residual, weight_scale):
    return pl.pallas_call(
        z_sum_kernel,
        in_specs=[VMEM] * (NZ + 1) + [pl.BlockSpec(memory_space=pltpu.SMEM)],
        out_specs=[VMEM] * 4,
        out_shape=[
            jax.ShapeDtypeStruct((OWN, COLS), jnp.float32),
            jax.ShapeDtypeStruct((OWN, COLS), jnp.bfloat16),
            jax.ShapeDtypeStruct((OWN, 128), jnp.float32),
            jax.ShapeDtypeStruct((OWN, 128), jnp.float32),
        ],
        compiler_params=PARAMS,
        name="z_sum",
    )(*parts, residual, weight_scale)


def norm_kernel(summed, a, b, c, d, gain, out):
    mean = (a[...] + b[...] + c[...] + d[...]) * (1.0 / (COLS * N_TENSOR))
    factor = lax.rsqrt(mean + 1e-05)[:, :1]
    out[...] = (summed[...] * factor * gain[...].astype(jnp.float32)).astype(jnp.bfloat16)


def norm(summed, squares, gain):
    return pl.pallas_call(
        norm_kernel,
        in_specs=[VMEM] * 6,
        out_specs=VMEM,
        out_shape=jax.ShapeDtypeStruct((OWN, COLS), jnp.bfloat16),
        compiler_params=PARAMS,
        name="norm",
    )(summed, *squares, gain)


def blocks_kernel(place, *refs):
    slabs, pick, rows, wide, narrow = refs[:8], *refs[8:]
    my_x, my_c = place[2], place[3]
    lane = lax.broadcasted_iota(jnp.int32, (SLAB, WIDTH), 1)
    for j, slab in enumerate(slabs):
        dx, dc = j // NC, j % NC
        t = lax.rem(my_x + NX - dx, NX) * NC + lax.rem(my_c + dc, NC)
        at = pl.ds(pl.multiple_of(t * SLAB, SLAB), SLAB)
        value = slab[...]
        rows[at, :] = value
        big = jnp.abs(value)
        for shift in (1, 2, 4, 8):
            up = pltpu.roll(big, WIDTH - shift, 1)
            down = pltpu.roll(big, shift, 1)
            big = jnp.maximum(big, jnp.where((lane & shift) == 0, up, down))
        wide[at, :] = big
    narrow[...] = jnp.dot(
        wide[...], pick[...], preferred_element_type=jnp.float32, precision=lax.Precision.HIGHEST
    )


def blocks(slabs, place):
    pick = np.zeros((WIDTH, WIDTH // 16), np.float32)
    pick[np.arange(WIDTH // 16) * 16, np.arange(WIDTH // 16)] = 1.0
    return pl.pallas_call(
        blocks_kernel,
        in_specs=[pl.BlockSpec(memory_space=pltpu.SMEM)] + [VMEM] * 9,
        out_specs=[VMEM] * 3,
        out_shape=[
            jax.ShapeDtypeStruct((ROWS, WIDTH), jnp.float32),
            jax.ShapeDtypeStruct((ROWS, WIDTH), jnp.float32),
            jax.ShapeDtypeStruct((ROWS, WIDTH // 16), jnp.float32),
        ],
        compiler_params=PARAMS,
        name="blocks",
    )(place, *slabs, jnp.asarray(pick))


def payload_kernel(rows, wide, narrow, peak, payload, block_scales):
    top = peak[0, 0]
    low = top / 64.0
    payload[...] = (6.0 * rows[...] / jnp.maximum(wide[...], low)).astype(jnp.bfloat16)
    block_scales[...] = 448.0 * jnp.maximum(narrow[...], low) / top


def encode(rows, wide, narrow, peak):
    return pl.pallas_call(
        payload_kernel,
        in_specs=[VMEM] * 4,
        out_specs=[VMEM] * 2,
        out_shape=[
            jax.ShapeDtypeStruct((ROWS, WIDTH), jnp.bfloat16),
            jax.ShapeDtypeStruct((ROWS, WIDTH // 16), jnp.float32),
        ],
        compiler_params=PARAMS,
        name="encode",
    )(rows, wide, narrow, peak)


def on_device(gate_pre, up_pre, down_codes, down_scales, weight_scale, residual, norm_gain):
    place = jnp.stack([lax.axis_index(a) for a in ("z", "y", "x", "c")]).astype(jnp.int32)
    tensor = (place[2] * NC + place[3]).reshape(1)
    inner = inner_transform(gate_pre, up_pre, tensor)
    one_row = lax.all_to_all(inner, ("z", "y"), 0, 0, tiled=True)
    turned = outer_transform(one_row)
    own = lax.all_to_all(turned, ("z", "y"), 0, 0, tiled=True)

    mine = [own, moved(own, "x", 1), moved(own, "x", 2), moved(own, "x", 3)]
    slabs = []
    for block in mine:
        slabs += [block, moved(block, "c", 1)]

    here, ahead, far_a, far_b, behind = product(slabs, down_codes, down_scales, place)
    first, second = moved(far_a, "y", 1), moved(far_b, "y", -1)
    ahead, behind = relay(ahead, first, behind, second)
    parts = y_sum(here, moved(ahead, "y", 1), moved(behind, "y", -1))
    parts = [parts[0]] + [moved(parts[d], "z", d) for d in (4, 3, 5, 2, 6, 1, 7)]
    summed, rounded, squares, peak = z_sum(parts, residual, weight_scale)
    squares = squares + moved(squares, "c", 1)
    normed = norm(
        summed,
        [squares, moved(squares, "x", 1), moved(squares, "x", 2), moved(squares, "x", 3)],
        norm_gain.reshape(1, COLS),
    )
    payload, block_scales = encode(*blocks(slabs, place), peak)
    return payload, block_scales, rounded, normed


def solution(mesh):
    mesh = Mesh(mesh.devices.reshape(NZ, NY, NX, NC), ("z", "y", "x", "c"))
    pipe, tensor = ("z", "y"), ("x", "c")
    in_specs = (
        P(None, pipe),
        P(None, pipe),
        P(pipe, tensor),
        P(pipe, tensor),
        P(),
        P(pipe, tensor),
        P(tensor),
    )
    out_specs = (P(None, pipe), P(None, pipe), P(pipe, tensor), P(pipe, tensor))
    return jax.shard_map(
        on_device, mesh=mesh, in_specs=in_specs, out_specs=out_specs, check_vma=False
    )
```

```python
import jax
import jax.numpy as jnp
from jax import lax
from jax.experimental import pallas as pl
from jax.experimental.pallas import tpu as pltpu
from jax.sharding import Mesh
from jax.sharding import PartitionSpec as P

NZ, NY, NX, NC = 8, 4, 4, 2
N_PIPE, N_TENSOR = NZ * NY, NX * NC
ROWS, GROUPS, INNER = 256, 13, 128
WIDTH = GROUPS * INNER
COLS = 2048
WIDE = COLS + 128
SLAB = ROWS // N_TENSOR
OWN = ROWS // N_PIPE
SIZES = {"z": NZ, "y": NY, "x": NX, "c": NC}
VMEM = pl.BlockSpec(memory_space=pltpu.VMEM)
SMEM = pl.BlockSpec(memory_space=pltpu.SMEM)
ANY = pl.BlockSpec(memory_space=pl.ANY)
HBM = pl.BlockSpec(memory_space=pltpu.HBM)
PARAMS = pltpu.CompilerParams(vmem_limit_bytes=16 * 1024 * 1024)
WEIGHT_PARAMS = pltpu.CompilerParams(vmem_limit_bytes=46 * 1024 * 1024)
def moved(block, axis, step):
    count = SIZES[axis]
    return lax.ppermute(block, axis, [(i, (i + step) % count) for i in range(count)])


def sign_matrix(order, scale):
    i = lax.broadcasted_iota(jnp.int32, (order, order), 0)
    j = lax.broadcasted_iota(jnp.int32, (order, order), 1)
    odd = i & j
    for shift in (4, 2, 1):
        odd = odd ^ (odd >> shift)
    return jnp.where((odd & 1) == 1, -scale, scale).astype(jnp.float32)


def inner_kernel(hidden, out):
    had = sign_matrix(INNER, 1.0 / 64.0).astype(jnp.bfloat16)
    for c in range(GROUPS):
        cols = slice(c * INNER, (c + 1) * INNER)
        out[:, cols] = jnp.dot(hidden[:, cols], had, preferred_element_type=jnp.float32)


def inner_transform(hidden):
    return pl.pallas_call(
        inner_kernel,
        in_specs=[VMEM],
        out_specs=VMEM,
        out_shape=jax.ShapeDtypeStruct((SLAB, WIDTH), jnp.float32),
        compiler_params=PARAMS,
        name="inner_transform",
    )(hidden)


def outer_kernel(block, out):
    out[...] = jnp.dot(
        sign_matrix(N_PIPE, 1.0),
        block[...],
        preferred_element_type=jnp.float32,
        precision=lax.Precision.HIGHEST,
    )


def outer_transform(block):
    return pl.pallas_call(
        outer_kernel,
        in_specs=[VMEM],
        out_specs=VMEM,
        out_shape=jax.ShapeDtypeStruct((N_PIPE, WIDTH), jnp.float32),
        compiler_params=PARAMS,
        name="outer_transform",
    )(block)


def stack_kernel(*refs):
    blocks, out = refs[:NX], refs[-1]
    for k, block in enumerate(blocks):
        out[k * SLAB : (k + 1) * SLAB, :] = block[...]


def stack(blocks, after):
    return pl.pallas_call(
        stack_kernel,
        in_specs=[VMEM] * NX + [ANY],
        out_specs=VMEM,
        out_shape=jax.ShapeDtypeStruct((NX * SLAB, WIDTH), jnp.float32),
        compiler_params=PARAMS,
        name="stack",
    )(*blocks, after)


def slab_list(halves, my_x, my_c):
    slabs = []
    for dc, half in enumerate(halves):
        for dx in range(NX):
            t = lax.rem(my_x + NX - dx, NX) * NC + lax.rem(my_c + dc, NC)
            slabs.append((half.at[pl.ds(dx * SLAB, SLAB)], t))
    return slabs


PART = 128
PARTS = WIDTH // PART


def decode_kernel(codes, scales, after, out, done, raw, raw_scales, wide, loaded, stored):
    def load(k):
        r = pl.ds(pl.multiple_of(k * PART, PART), PART)
        return pltpu.make_async_copy(codes.at[r], raw.at[r], loaded.at[k])

    def store(k):
        r = pl.ds(pl.multiple_of(k * PART, PART), PART)
        return pltpu.make_async_copy(raw.at[r], out.at[r], stored.at[k])

    load_scales = pltpu.make_async_copy(scales, raw_scales, loaded.at[PARTS])
    load_scales.start()
    for k in range(PARTS):
        load(k).start()
    done[...] = jnp.zeros((8, 128), jnp.float32)
    load_scales.wait()
    wide[...] = raw_scales[...].astype(jnp.float32)

    @pl.loop(0, PARTS)
    def _(k):
        load(k).wait()
        rows = wide[pl.ds(pl.multiple_of(k * 8, 8), 8), :]
        for i in range(PART // 16):
            at = pl.ds(pl.multiple_of(k * PART + i * 16, 16), 16)
            s = jnp.broadcast_to(rows[i : i + 1, :], (16, COLS)).astype(jnp.bfloat16)
            raw[at, :] = raw[at, :] * s
        store(k).start()

    for k in range(PARTS):
        store(k).wait()


def decode(codes, scales, after):
    return pl.pallas_call(
        decode_kernel,
        in_specs=[HBM, HBM, ANY],
        out_specs=[HBM, VMEM],
        out_shape=[
            jax.ShapeDtypeStruct((WIDTH, COLS), jnp.bfloat16),
            jax.ShapeDtypeStruct((8, 128), jnp.float32),
        ],
        scratch_shapes=[
            pltpu.VMEM((WIDTH, COLS), jnp.bfloat16),
            pltpu.VMEM((WIDTH // 16, COLS), jnp.bfloat16),
            pltpu.VMEM((WIDTH // 16, COLS), jnp.float32),
            pltpu.SemaphoreType.DMA((PARTS + 1,)),
            pltpu.SemaphoreType.DMA((PARTS,)),
        ],
        compiler_params=WEIGHT_PARAMS,
        cost_estimate=pl.CostEstimate(flops=WIDTH * COLS, bytes_accessed=14 << 20, transcendentals=0),
        name="decode",
    )(codes, scales, after)


BN = 512
TILES = COLS // BN


def product_kernel(place, *refs):
    halves, weight, outs, (rows32, rows16, tiles, sems) = refs[:2], refs[2], refs[3:8], refs[8:]
    copies = [
        pltpu.make_async_copy(weight.at[:, pl.ds(k * BN, BN)], tiles.at[k], sems.at[k])
        for k in range(TILES)
    ]
    for copy in copies:
        copy.start()
    my_z, my_y, my_x, my_c = place[0], place[1], place[2], place[3]
    top = jnp.zeros((8, WIDTH), jnp.float32)
    for slab, z in slab_list(halves, my_x, my_c):
        z_step = lax.rem(z - my_z + NZ, NZ)
        for y in range(NY):
            y_step = lax.rem(y - my_y + NY, NY)
            piece = slab[y * OWN : (y + 1) * OWN, :]
            top = jnp.maximum(top, jnp.abs(piece))
            at = pl.multiple_of(y_step * (NZ * OWN) + z_step * OWN, OWN)
            rows32[pl.ds(at, OWN), :] = piece
    rows16[...] = rows32[...].astype(jnp.bfloat16)
    peak = jnp.full((8, 128), jnp.max(top), jnp.float32)
    for out in outs:
        for k in range(out.shape[0] // 8):
            out[k * 8 : (k + 1) * 8, COLS:] = peak

    for k, copy in enumerate(copies):
        copy.wait()
        total = jnp.dot(rows16[...], tiles[k], preferred_element_type=jnp.float32)
        at = 0
        for out in outs:
            out[:, k * BN : (k + 1) * BN] = total[at : at + out.shape[0], :]
            at += out.shape[0]


def product(slabs, weight, place):
    sizes = [64, 64, 32, 32, 64]
    return pl.pallas_call(
        product_kernel,
        in_specs=[SMEM] + [VMEM] * 2 + [HBM],
        out_specs=[VMEM] * 5,
        out_shape=[jax.ShapeDtypeStruct((n, WIDE), jnp.float32) for n in sizes],
        scratch_shapes=[
            pltpu.VMEM((ROWS, WIDTH), jnp.float32),
            pltpu.VMEM((ROWS, WIDTH), jnp.bfloat16),
            pltpu.VMEM((TILES, WIDTH, BN), jnp.bfloat16),
            pltpu.SemaphoreType.DMA((TILES,)),
        ],
        compiler_params=WEIGHT_PARAMS,
        name="product",
    )(place, *slabs, weight)


def relay_kernel(a, first, b, second, out_a, out_b):
    out_a[...] = a[...]
    out_b[...] = b[...]
    out_a[:32, :COLS] += first[:, :COLS]
    out_b[32:, :COLS] += second[:, :COLS]
    other = jnp.maximum(first[:, COLS:], second[:, COLS:])
    out_a[:32, COLS:] = jnp.maximum(a[:32, COLS:], other)
    out_b[:32, COLS:] = jnp.maximum(b[:32, COLS:], other)


def relay(a, first, b, second):
    shape = jax.ShapeDtypeStruct((64, WIDE), jnp.float32)
    return pl.pallas_call(
        relay_kernel,
        in_specs=[VMEM] * 4,
        out_specs=[VMEM] * 2,
        out_shape=[shape] * 2,
        compiler_params=PARAMS,
        name="relay",
    )(a, first, b, second)


def y_sum_kernel(a, b, c, after, *outs):
    top = jnp.maximum(jnp.maximum(a[:8, COLS:], b[:8, COLS:]), c[:8, COLS:])
    for k, out in enumerate(outs):
        r = slice(k * OWN, (k + 1) * OWN)
        out[:, :COLS] = a[r, :COLS] + b[r, :COLS] + c[r, :COLS]
        out[:, COLS:] = top


def y_sum(a, b, c, after):
    return pl.pallas_call(
        y_sum_kernel,
        in_specs=[VMEM] * 3 + [ANY],
        out_specs=[VMEM] * NZ,
        out_shape=[jax.ShapeDtypeStruct((OWN, WIDE), jnp.float32)] * NZ,
        compiler_params=PARAMS,
        name="y_sum",
    )(a, b, c, after)


def z_sum_kernel(*refs):
    parts, residual, scale, summed, rounded, squares, top = refs[:NZ], *refs[NZ:]
    total = parts[0][:, :COLS]
    peak = parts[0][:, COLS:]
    for part in parts[1:]:
        total += part[:, :COLS]
        peak = jnp.maximum(peak, part[:, COLS:])
    total = residual[...].astype(jnp.float32) + total * scale[0]
    summed[...] = total
    rounded[...] = total.astype(jnp.bfloat16)
    squares[...] = jnp.broadcast_to(jnp.sum(total * total, axis=1, keepdims=True), (OWN, 128))
    top[...] = peak


def z_sum(parts, residual, weight_scale):
    return pl.pallas_call(
        z_sum_kernel,
        in_specs=[VMEM] * (NZ + 1) + [SMEM],
        out_specs=[VMEM] * 4,
        out_shape=[
            jax.ShapeDtypeStruct((OWN, COLS), jnp.float32),
            jax.ShapeDtypeStruct((OWN, COLS), jnp.bfloat16),
            jax.ShapeDtypeStruct((OWN, 128), jnp.float32),
            jax.ShapeDtypeStruct((OWN, 128), jnp.float32),
        ],
        compiler_params=PARAMS,
        name="z_sum",
    )(*parts, residual, weight_scale)


def norm_kernel(summed, a, b, c, d, gain, after, out):
    mean = (a[...] + b[...] + c[...] + d[...]) * (1.0 / (COLS * N_TENSOR))
    factor = lax.rsqrt(mean + 1e-05)[:, :1]
    out[...] = (summed[...] * factor * gain[...].astype(jnp.float32)).astype(jnp.bfloat16)


def norm(summed, squares, gain, after):
    return pl.pallas_call(
        norm_kernel,
        in_specs=[VMEM] * 6 + [ANY],
        out_specs=VMEM,
        out_shape=jax.ShapeDtypeStruct((OWN, COLS), jnp.bfloat16),
        compiler_params=PARAMS,
        name="norm",
    )(summed, *squares, gain, after)


def split3(value):
    parts = []
    for _ in range(3):
        part = value.astype(jnp.bfloat16)
        parts.append(part)
        value = value - part.astype(jnp.float32)
    return parts


def blocks_kernel(place, *refs):
    halves, after, narrow, factor, wide = refs[:2], *refs[2:]
    my_x, my_c = place[2], place[3]
    lane = lax.broadcasted_iota(jnp.int32, (SLAB, WIDTH), 1)
    for slab, t in slab_list(halves, my_x, my_c):
        at = pl.ds(pl.multiple_of(t * SLAB, SLAB), SLAB)
        big = jnp.abs(slab[...])
        for shift in (1, 2, 4, 8):
            up = pltpu.roll(big, WIDTH - shift, 1)
            down = pltpu.roll(big, shift, 1)
            big = jnp.maximum(big, jnp.where((lane & shift) == 0, up, down))
        wide[at, :] = big
        factor[at, :] = 6.0 / big
    block = lax.broadcasted_iota(jnp.int32, (WIDTH // 16, WIDTH), 0)
    unit = lax.broadcasted_iota(jnp.int32, (WIDTH // 16, WIDTH), 1)
    first = jnp.where(unit == 16 * block, 1.0, 0.0).astype(jnp.bfloat16)
    narrow[...] = sum(
        lax.dot_general(first, part, (((1,), (1,)), ((), ())), preferred_element_type=jnp.float32)
        for part in split3(wide[...])
    )


def blocks(slabs, place, after):
    return pl.pallas_call(
        blocks_kernel,
        in_specs=[SMEM] + [VMEM] * 2 + [ANY],
        out_specs=[VMEM] * 2,
        out_shape=[
            jax.ShapeDtypeStruct((WIDTH // 16, ROWS), jnp.float32),
            jax.ShapeDtypeStruct((ROWS, WIDTH), jnp.float32),
        ],
        scratch_shapes=[pltpu.VMEM((ROWS, WIDTH), jnp.float32)],
        compiler_params=PARAMS,
        name="blocks",
    )(place, *slabs, after)


def encode_kernel(place, *refs):
    halves, narrow, factor, peak, payload, block_scales, done = refs[:2], *refs[2:]
    done[...] = peak[...]
    my_x, my_c = place[2], place[3]
    top = peak[...]
    low = top / 64.0
    most = (6.0 / low)[:1, :1]
    block_scales[...] = jnp.maximum(narrow[...], low[:1, :1]) * (448.0 / top)[:1, :1]
    for slab, t in slab_list(halves, my_x, my_c):
        at = pl.ds(pl.multiple_of(t * SLAB, SLAB), SLAB)
        payload[at, :] = (slab[...] * jnp.minimum(factor[at, :], most)).astype(jnp.bfloat16)


def encode(slabs, place, narrow, factor, peak):
    return pl.pallas_call(
        encode_kernel,
        in_specs=[SMEM] + [VMEM] * 5,
        out_specs=[VMEM] * 3,
        out_shape=[
            jax.ShapeDtypeStruct((ROWS, WIDTH), jnp.bfloat16),
            jax.ShapeDtypeStruct((WIDTH // 16, ROWS), jnp.float32),
            jax.ShapeDtypeStruct((OWN, 128), jnp.float32),
        ],
        compiler_params=PARAMS,
        name="encode",
    )(place, *slabs, narrow, factor, peak)


def on_device(gate_pre, up_pre, down_codes, down_scales, weight_scale, residual, norm_gain):
    place = jnp.stack([lax.axis_index(a) for a in ("z", "y", "x", "c")]).astype(jnp.int32)
    first_row = (place[2] * NC + place[3]) * SLAB
    gate = lax.dynamic_slice_in_dim(gate_pre, first_row, SLAB, 0).astype(jnp.float32)
    up = lax.dynamic_slice_in_dim(up_pre, first_row, SLAB, 0).astype(jnp.float32)
    inner = inner_transform((gate / (1.0 + jnp.exp(-gate)) * up).astype(jnp.bfloat16))
    one_row = lax.all_to_all(inner, ("z", "y"), 0, 0, tiled=True)
    turned = outer_transform(one_row)
    own = lax.all_to_all(turned, ("z", "y"), 0, 0, tiled=True)

    mine = [moved(own, "x", k) for k in (1, 2, 3)]
    weight, done = decode(down_codes, down_scales, own)
    mine = stack([own] + mine, done)
    slabs = [mine, moved(mine, "c", 1)]
    here, ahead, far_a, far_b, behind = product(slabs, weight, place)
    first, second = moved(far_a, "y", 1), moved(far_b, "y", -1)
    ahead, behind = relay(ahead, first, behind, second)
    narrow, factor = blocks(slabs, place, ahead)
    parts = y_sum(here, moved(ahead, "y", 1), moved(behind, "y", -1), narrow)
    parts = [parts[0]] + [moved(parts[d], "z", d) for d in (4, 3, 5, 2, 6, 1, 7)]
    summed, rounded, squares, peak = z_sum(parts, residual, weight_scale)
    squares = squares + moved(squares, "c", 1)
    others = [moved(squares, "x", 1), moved(squares, "x", 2), moved(squares, "x", 3)]
    payload, block_scales, done = encode(slabs, place, narrow, factor, peak)
    normed = norm(summed, [squares] + others, norm_gain.reshape(1, COLS), done)
    return payload, block_scales.T, rounded, normed


def solution(mesh):
    mesh = Mesh(mesh.devices.reshape(NZ, NY, NX, NC), ("z", "y", "x", "c"))
    pipe, tensor = ("z", "y"), ("x", "c")
    in_specs = (
        P(None, pipe),
        P(None, pipe),
        P(pipe, tensor),
        P(pipe, tensor),
        P(),
        P(pipe, tensor),
        P(tensor),
    )
    out_specs = (P(None, pipe), P(None, pipe), P(pipe, tensor), P(pipe, tensor))
    return jax.shard_map(
        on_device, mesh=mesh, in_specs=in_specs, out_specs=out_specs, check_vma=False
    )
```

```python
import jax
import jax.numpy as jnp
from jax import lax
from jax.experimental import pallas as pl
from jax.experimental.pallas import tpu as pltpu
from jax.sharding import Mesh
from jax.sharding import PartitionSpec as P

NZ, NY, NX, NC = 8, 4, 4, 2
N_PIPE, N_TENSOR = NZ * NY, NX * NC
ROWS, GROUPS, INNER = 256, 13, 128
WIDTH = GROUPS * INNER
COLS = 2048
WIDE = COLS + 128
SLAB = ROWS // N_TENSOR
OWN = ROWS // N_PIPE
SIZES = {"z": NZ, "y": NY, "x": NX, "c": NC}
VMEM = pl.BlockSpec(memory_space=pltpu.VMEM)
SMEM = pl.BlockSpec(memory_space=pltpu.SMEM)
ANY = pl.BlockSpec(memory_space=pl.ANY)
HBM = pl.BlockSpec(memory_space=pltpu.HBM)
PARAMS = pltpu.CompilerParams(vmem_limit_bytes=16 * 1024 * 1024)
DECODE_PARAMS = pltpu.CompilerParams(vmem_limit_bytes=50 * 1024 * 1024)
WEIGHT_PARAMS = pltpu.CompilerParams(vmem_limit_bytes=46 * 1024 * 1024)
def moved(block, axis, step):
    count = SIZES[axis]
    return lax.ppermute(block, axis, [(i, (i + step) % count) for i in range(count)])


def sign_matrix(order, scale):
    i = lax.broadcasted_iota(jnp.int32, (order, order), 0)
    j = lax.broadcasted_iota(jnp.int32, (order, order), 1)
    odd = i & j
    for shift in (4, 2, 1):
        odd = odd ^ (odd >> shift)
    return jnp.where((odd & 1) == 1, -scale, scale).astype(jnp.float32)


def inner_kernel(hidden, out):
    had = sign_matrix(INNER, 1.0 / 64.0).astype(jnp.bfloat16)
    for c in range(GROUPS):
        cols = slice(c * INNER, (c + 1) * INNER)
        out[:, cols] = jnp.dot(hidden[:, cols], had, preferred_element_type=jnp.float32)


def inner_transform(hidden):
    return pl.pallas_call(
        inner_kernel,
        in_specs=[VMEM],
        out_specs=VMEM,
        out_shape=jax.ShapeDtypeStruct((SLAB, WIDTH), jnp.float32),
        compiler_params=PARAMS,
        name="inner_transform",
    )(hidden)


def outer_kernel(block, out):
    out[...] = jnp.dot(
        sign_matrix(N_PIPE, 1.0),
        block[...],
        preferred_element_type=jnp.float32,
        precision=lax.Precision.HIGHEST,
    )


def outer_transform(block):
    return pl.pallas_call(
        outer_kernel,
        in_specs=[VMEM],
        out_specs=VMEM,
        out_shape=jax.ShapeDtypeStruct((N_PIPE, WIDTH), jnp.float32),
        compiler_params=PARAMS,
        name="outer_transform",
    )(block)


def hand_on_kernel(block, after, out):
    out[...] = block[...]


def hand_on(block, after):
    return pl.pallas_call(
        hand_on_kernel,
        in_specs=[VMEM, ANY],
        out_specs=VMEM,
        out_shape=jax.ShapeDtypeStruct((SLAB, WIDTH), jnp.float32),
        compiler_params=PARAMS,
        name="hand_on",
    )(block, after)


def slab_place(j, my_x, my_c):
    return lax.rem(my_x + NX - j % NX, NX) * NC + lax.rem(my_c + j // NX, NC)


PART = 128
PARTS = WIDTH // PART


def decode_kernel(codes, scales, after, out, done, raw, raw_scales, wide, loaded, stored):
    def load(k):
        r = pl.ds(pl.multiple_of(k * PART, PART), PART)
        return pltpu.make_async_copy(codes.at[r], raw.at[r], loaded.at[k])

    def store(k):
        r = pl.ds(pl.multiple_of(k * PART, PART), PART)
        return pltpu.make_async_copy(raw.at[r], out.at[r], stored.at[k])

    load_scales = pltpu.make_async_copy(scales, raw_scales, loaded.at[PARTS])
    load_scales.start()
    for k in range(PARTS):
        load(k).start()
    done[...] = jnp.zeros((8, 128), jnp.float32)
    load_scales.wait()
    wide[...] = raw_scales[...].astype(jnp.float32)

    @pl.loop(0, PARTS)
    def _(k):
        load(k).wait()
        rows = wide[pl.ds(pl.multiple_of(k * 8, 8), 8), :]
        for i in range(PART // 16):
            at = pl.ds(pl.multiple_of(k * PART + i * 16, 16), 16)
            s = jnp.broadcast_to(rows[i : i + 1, :], (16, COLS)).astype(jnp.bfloat16)
            raw[at, :] = raw[at, :] * s
        store(k).start()

    for k in range(PARTS):
        store(k).wait()


def decode(codes, scales, after):
    return pl.pallas_call(
        decode_kernel,
        in_specs=[HBM, HBM, ANY],
        out_specs=[HBM, VMEM],
        out_shape=[
            jax.ShapeDtypeStruct((WIDTH, COLS), jnp.bfloat16),
            jax.ShapeDtypeStruct((8, 128), jnp.float32),
        ],
        scratch_shapes=[
            pltpu.VMEM((WIDTH, COLS), jnp.bfloat16),
            pltpu.VMEM((WIDTH // 16, COLS), jnp.bfloat16),
            pltpu.VMEM((WIDTH // 16, COLS), jnp.float32),
            pltpu.SemaphoreType.DMA((PARTS + 1,)),
            pltpu.SemaphoreType.DMA((PARTS,)),
        ],
        compiler_params=DECODE_PARAMS,
        cost_estimate=pl.CostEstimate(flops=WIDTH * COLS, bytes_accessed=14 << 20, transcendentals=0),
        name="decode",
    )(codes, scales, after)


BN = 512
TILES = COLS // BN
HALF = 32
Z_ORDER = (4, 3, 5, 2, 6, 1, 7, 0)


def product_kernel(place, *refs):
    slabs, weight, outs, (rows32, rows16, tiles, sems) = refs[:8], refs[8], refs[9:17], refs[17:]
    copies = [
        pltpu.make_async_copy(weight.at[:, pl.ds(k * BN, BN)], tiles.at[k], sems.at[k])
        for k in range(TILES)
    ]
    for copy in copies:
        copy.start()
    my_z, my_y, my_x, my_c = place[0], place[1], place[2], place[3]
    biggest = jnp.zeros((8, WIDTH), jnp.float32)
    for j, slab in enumerate(slabs):
        z = slab_place(j, my_x, my_c)
        z_step = lax.rem(z - my_z + NZ, NZ)
        z_at = jnp.int32(0)
        for k, step in enumerate(Z_ORDER):
            z_at = jnp.where(z_step == step, k, z_at)
        for y in range(NY):
            y_step = lax.rem(y - my_y + NY, NY)
            piece = slab[y * OWN : (y + 1) * OWN, :]
            biggest = jnp.maximum(biggest, jnp.abs(piece))
            at = pl.multiple_of(y_step * (NZ * OWN) + z_at * OWN, OWN)
            rows32[pl.ds(at, OWN), :] = piece
    rows16[...] = rows32[...].astype(jnp.bfloat16)
    top = jnp.full((8, 128), jnp.max(biggest), jnp.float32)
    for out in outs:
        for k in range(HALF // 8):
            out[k * 8 : (k + 1) * 8, COLS:] = top
    for k, copy in enumerate(copies):
        copy.wait()
        total = jnp.dot(rows16[...], tiles[k], preferred_element_type=jnp.float32)
        for i, out in enumerate(outs):
            out[:, k * BN : (k + 1) * BN] = total[i * HALF : (i + 1) * HALF, :]


def product(slabs, weight, place):
    return pl.pallas_call(
        product_kernel,
        in_specs=[SMEM] + [VMEM] * 8 + [HBM],
        out_specs=[VMEM] * 8,
        out_shape=[jax.ShapeDtypeStruct((HALF, WIDE), jnp.float32)] * 8,
        scratch_shapes=[
            pltpu.VMEM((ROWS, WIDTH), jnp.float32),
            pltpu.VMEM((ROWS, WIDTH), jnp.bfloat16),
            pltpu.VMEM((TILES, WIDTH, BN), jnp.bfloat16),
            pltpu.SemaphoreType.DMA((TILES,)),
        ],
        compiler_params=WEIGHT_PARAMS,
        name="product",
    )(place, *slabs, weight)


def relay_kernel(own, arrived, out):
    out[:, :COLS] = own[:, :COLS] + arrived[:, :COLS]
    out[:, COLS:] = jnp.maximum(own[:, COLS:], arrived[:, COLS:])


def relay(own, arrived):
    return pl.pallas_call(
        relay_kernel,
        in_specs=[VMEM] * 2,
        out_specs=VMEM,
        out_shape=jax.ShapeDtypeStruct((HALF, WIDE), jnp.float32),
        compiler_params=PARAMS,
        name="relay",
    )(own, arrived)


def y_sum_kernel(a, b, c, after, *outs):
    top = jnp.maximum(jnp.maximum(a[:8, COLS:], b[:8, COLS:]), c[:8, COLS:])
    for k, out in enumerate(outs):
        r = slice(k * OWN, (k + 1) * OWN)
        out[:, :COLS] = a[r, :COLS] + b[r, :COLS] + c[r, :COLS]
        out[:, COLS:] = top


def y_sum(a, b, c, after):
    return pl.pallas_call(
        y_sum_kernel,
        in_specs=[VMEM] * 3 + [ANY],
        out_specs=[VMEM] * (HALF // OWN),
        out_shape=[jax.ShapeDtypeStruct((OWN, WIDE), jnp.float32)] * (HALF // OWN),
        compiler_params=PARAMS,
        name="y_sum",
    )(a, b, c, after)


def z_sum_kernel(*refs):
    parts, residual, scale, after, summed, rounded, squares, top = refs[:NZ], *refs[NZ:]
    total = parts[0][:, :COLS]
    peak = parts[0][:, COLS:]
    for part in parts[1:]:
        total += part[:, :COLS]
        peak = jnp.maximum(peak, part[:, COLS:])
    total = residual[...].astype(jnp.float32) + total * scale[0]
    summed[...] = total
    rounded[...] = total.astype(jnp.bfloat16)
    squares[...] = jnp.broadcast_to(jnp.sum(total * total, axis=1, keepdims=True), (OWN, 128))
    top[...] = peak


def z_sum(parts, residual, weight_scale, after):
    return pl.pallas_call(
        z_sum_kernel,
        in_specs=[VMEM] * (NZ + 1) + [SMEM, ANY],
        out_specs=[VMEM] * 4,
        out_shape=[
            jax.ShapeDtypeStruct((OWN, COLS), jnp.float32),
            jax.ShapeDtypeStruct((OWN, COLS), jnp.bfloat16),
            jax.ShapeDtypeStruct((OWN, 128), jnp.float32),
            jax.ShapeDtypeStruct((OWN, 128), jnp.float32),
        ],
        compiler_params=PARAMS,
        name="z_sum",
    )(*parts, residual, weight_scale, after)


def norm_kernel(summed, a, b, c, d, gain, after, out):
    mean = (a[...] + b[...] + c[...] + d[...]) * (1.0 / (COLS * N_TENSOR))
    factor = lax.rsqrt(mean + 1e-05)[:, :1]
    out[...] = (summed[...] * factor * gain[...].astype(jnp.float32)).astype(jnp.bfloat16)


def norm(summed, squares, gain, after):
    return pl.pallas_call(
        norm_kernel,
        in_specs=[VMEM] * 6 + [ANY],
        out_specs=VMEM,
        out_shape=jax.ShapeDtypeStruct((OWN, COLS), jnp.bfloat16),
        compiler_params=PARAMS,
        name="norm",
    )(summed, *squares, gain, after)


def split3(value):
    parts = []
    for _ in range(3):
        part = value.astype(jnp.bfloat16)
        parts.append(part)
        value = value - part.astype(jnp.float32)
    return parts


def block_maxima(rows, factor, wide):
    lane = lax.broadcasted_iota(jnp.int32, (SLAB, WIDTH), 1)
    for k, slab in enumerate(rows):
        at = slice(k * SLAB, (k + 1) * SLAB)
        big = jnp.abs(slab[...])
        for shift in (1, 2, 4, 8):
            up = pltpu.roll(big, WIDTH - shift, 1)
            down = pltpu.roll(big, shift, 1)
            big = jnp.maximum(big, jnp.where((lane & shift) == 0, up, down))
        wide[at, :] = big
        factor[at, :] = 6.0 / big
    block = lax.broadcasted_iota(jnp.int32, (WIDTH, WIDTH // 16), 1)
    unit = lax.broadcasted_iota(jnp.int32, (WIDTH, WIDTH // 16), 0)
    first = jnp.where(unit == 16 * block, 1.0, 0.0).astype(jnp.bfloat16)
    return sum(
        jnp.dot(part, first, preferred_element_type=jnp.float32) for part in split3(wide[...])
    )


def mine_kernel(*refs):
    rows, (after, narrow, factor, wide) = refs[:4], refs[4:]
    narrow[...] = block_maxima(rows, factor, wide)


def theirs_kernel(place, *refs):
    rows, (mine, after, narrow, factor, wide, all_rows) = refs[:4], refs[4:]
    maxima = block_maxima(rows, factor, wide)
    for dc, half in enumerate((mine[...], maxima)):
        for dx in range(NX):
            t = slab_place(dc * NX + dx, place[2], place[3])
            at = pl.ds(pl.multiple_of(t * SLAB, SLAB), SLAB)
            all_rows[at, :] = half[dx * SLAB : (dx + 1) * SLAB, :]
    narrow[...] = all_rows[...].T


def mine_blocks(rows, after):
    return pl.pallas_call(
        mine_kernel,
        in_specs=[VMEM] * 4 + [ANY],
        out_specs=[VMEM] * 2,
        out_shape=[
            jax.ShapeDtypeStruct((ROWS // 2, WIDTH // 16), jnp.float32),
            jax.ShapeDtypeStruct((ROWS // 2, WIDTH), jnp.float32),
        ],
        scratch_shapes=[pltpu.VMEM((ROWS // 2, WIDTH), jnp.float32)],
        compiler_params=PARAMS,
        name="mine_blocks",
    )(*rows, after)


def theirs_blocks(place, rows, mine, after):
    return pl.pallas_call(
        theirs_kernel,
        in_specs=[SMEM] + [VMEM] * 5 + [ANY],
        out_specs=[VMEM] * 2,
        out_shape=[
            jax.ShapeDtypeStruct((WIDTH // 16, ROWS), jnp.float32),
            jax.ShapeDtypeStruct((ROWS // 2, WIDTH), jnp.float32),
        ],
        scratch_shapes=[
            pltpu.VMEM((ROWS // 2, WIDTH), jnp.float32),
            pltpu.VMEM((ROWS, WIDTH // 16), jnp.float32),
        ],
        compiler_params=PARAMS,
        name="theirs_blocks",
    )(place, *rows, mine, after)


def encode_kernel(place, *refs):
    slabs, factors, (narrow, peak, payload, block_scales, done) = refs[:8], refs[8:10], refs[10:]
    done[...] = peak[...]
    my_x, my_c = place[2], place[3]
    top = peak[...]
    low = top / 64.0
    most = (6.0 / low)[:1, :1]
    block_scales[...] = jnp.maximum(narrow[...], low[:1, :1]) * (448.0 / top)[:1, :1]
    for j, slab in enumerate(slabs):
        at = pl.ds(pl.multiple_of(slab_place(j, my_x, my_c) * SLAB, SLAB), SLAB)
        k = j % NX * SLAB
        value = slab[...] * jnp.minimum(factors[j // NX][k : k + SLAB, :], most)
        payload[at, :] = value.astype(jnp.bfloat16)


def encode(slabs, factors, place, narrow, peak):
    return pl.pallas_call(
        encode_kernel,
        in_specs=[SMEM] + [VMEM] * 12,
        out_specs=[VMEM] * 3,
        out_shape=[
            jax.ShapeDtypeStruct((ROWS, WIDTH), jnp.bfloat16),
            jax.ShapeDtypeStruct((WIDTH // 16, ROWS), jnp.float32),
            jax.ShapeDtypeStruct((OWN, 128), jnp.float32),
        ],
        compiler_params=PARAMS,
        name="encode",
    )(place, *slabs, *factors, narrow, peak)


def on_device(gate_pre, up_pre, down_codes, down_scales, weight_scale, residual, norm_gain):
    place = jnp.stack([lax.axis_index(a) for a in ("z", "y", "x", "c")]).astype(jnp.int32)
    first_row = (place[2] * NC + place[3]) * SLAB
    gate = lax.dynamic_slice_in_dim(gate_pre, first_row, SLAB, 0).astype(jnp.float32)
    up = lax.dynamic_slice_in_dim(up_pre, first_row, SLAB, 0).astype(jnp.float32)
    inner = inner_transform((gate / (1.0 + jnp.exp(-gate)) * up).astype(jnp.bfloat16))
    one_row = lax.all_to_all(inner, ("z", "y"), 0, 0, tiled=True)
    turned = outer_transform(one_row)
    own = lax.all_to_all(turned, ("z", "y"), 0, 0, tiled=True)

    mine = [moved(own, "x", k) for k in (1, 2, 3)]
    weight, done = decode(down_codes, down_scales, own)
    mine = [own] + [hand_on(block, done) for block in mine]
    theirs = [moved(block, "c", 1) for block in mine]
    slabs = mine + theirs
    here_a, here_b, ahead_a, ahead_b, far_a, far_b, behind_a, behind_b = product(slabs, weight, place)
    first, second = moved(far_a, "y", 1), moved(far_b, "y", -1)
    ahead_b, behind_a = moved(ahead_b, "y", 1), moved(behind_a, "y", -1)
    ahead_a, behind_b = relay(ahead_a, first), relay(behind_b, second)
    mine_most, mine_factor = mine_blocks(mine, behind_b)
    sums_a = y_sum(here_a, moved(ahead_a, "y", 1), behind_a, mine_most)
    sums_b = y_sum(here_b, ahead_b, moved(behind_b, "y", -1), mine_most)
    sums = [*sums_a, *sums_b]
    parts = [moved(part, "z", step) if step else part for part, step in zip(sums, Z_ORDER)]
    narrow, theirs_factor = theirs_blocks(place, theirs, mine_most, sums_b[0])
    summed, rounded, squares, peak = z_sum(parts, residual, weight_scale, narrow)
    squares = squares + moved(squares, "c", 1)
    others = [moved(squares, "x", 1), moved(squares, "x", 2), moved(squares, "x", 3)]
    payload, block_scales, done = encode(
        slabs, (mine_factor, theirs_factor), place, narrow, peak
    )
    normed = norm(summed, [squares] + others, norm_gain.reshape(1, COLS), done)
    return payload, block_scales.T, rounded, normed


def solution(mesh):
    mesh = Mesh(mesh.devices.reshape(NZ, NY, NX, NC), ("z", "y", "x", "c"))
    pipe, tensor = ("z", "y"), ("x", "c")
    in_specs = (
        P(None, pipe),
        P(None, pipe),
        P(pipe, tensor),
        P(pipe, tensor),
        P(),
        P(pipe, tensor),
        P(tensor),
    )
    out_specs = (P(None, pipe), P(None, pipe), P(pipe, tensor), P(pipe, tensor))
    return jax.shard_map(
        on_device, mesh=mesh, in_specs=in_specs, out_specs=out_specs, check_vma=False
    )
```

```python
import jax
import jax.numpy as jnp
from jax import lax
from jax.experimental import pallas as pl
from jax.experimental.pallas import tpu as pltpu
from jax.sharding import Mesh
from jax.sharding import PartitionSpec as P

NZ, NY, NX, NC = 8, 4, 4, 2
N_PIPE, N_TENSOR = NZ * NY, NX * NC
ROWS, GROUPS, INNER = 256, 13, 128
WIDTH = GROUPS * INNER
COLS = 2048
WIDE = COLS + 128
SLAB = ROWS // N_TENSOR
OWN = ROWS // N_PIPE
SIZES = {"z": NZ, "y": NY, "x": NX, "c": NC}
VMEM = pl.BlockSpec(memory_space=pltpu.VMEM)
SMEM = pl.BlockSpec(memory_space=pltpu.SMEM)
ANY = pl.BlockSpec(memory_space=pl.ANY)
HBM = pl.BlockSpec(memory_space=pltpu.HBM)
PARAMS = pltpu.CompilerParams(vmem_limit_bytes=16 * 1024 * 1024)
DECODE_PARAMS = pltpu.CompilerParams(vmem_limit_bytes=50 * 1024 * 1024)
WEIGHT_PARAMS = pltpu.CompilerParams(vmem_limit_bytes=46 * 1024 * 1024)
def moved(block, axis, step):
    count = SIZES[axis]
    return lax.ppermute(block, axis, [(i, (i + step) % count) for i in range(count)])


def sign_matrix(order, scale):
    i = lax.broadcasted_iota(jnp.int32, (order, order), 0)
    j = lax.broadcasted_iota(jnp.int32, (order, order), 1)
    odd = i & j
    for shift in (4, 2, 1):
        odd = odd ^ (odd >> shift)
    return jnp.where((odd & 1) == 1, -scale, scale).astype(jnp.float32)


def inner_kernel(hidden, out):
    had = sign_matrix(INNER, 1.0 / 64.0).astype(jnp.bfloat16)
    for c in range(GROUPS):
        cols = slice(c * INNER, (c + 1) * INNER)
        out[:, cols] = jnp.dot(hidden[:, cols], had, preferred_element_type=jnp.float32)


def inner_transform(hidden):
    return pl.pallas_call(
        inner_kernel,
        in_specs=[VMEM],
        out_specs=VMEM,
        out_shape=jax.ShapeDtypeStruct((SLAB, WIDTH), jnp.float32),
        compiler_params=PARAMS,
        name="inner_transform",
    )(hidden)


def outer_kernel(block, out):
    out[...] = jnp.dot(
        sign_matrix(N_PIPE, 1.0),
        block[...],
        preferred_element_type=jnp.float32,
        precision=lax.Precision.HIGHEST,
    )


def outer_transform(block):
    return pl.pallas_call(
        outer_kernel,
        in_specs=[VMEM],
        out_specs=VMEM,
        out_shape=jax.ShapeDtypeStruct((N_PIPE, WIDTH), jnp.float32),
        compiler_params=PARAMS,
        name="outer_transform",
    )(block)


def hand_on_kernel(block, after, out):
    out[...] = block[...]


def hand_on(block, after):
    return pl.pallas_call(
        hand_on_kernel,
        in_specs=[VMEM, ANY],
        out_specs=VMEM,
        out_shape=jax.ShapeDtypeStruct((SLAB, WIDTH), jnp.float32),
        compiler_params=PARAMS,
        name="hand_on",
    )(block, after)


def slab_place(j, my_x, my_c):
    return lax.rem(my_x + NX - j % NX, NX) * NC + lax.rem(my_c + j // NX, NC)


PART = 128
PARTS = WIDTH // PART


def decode_kernel(codes, scales, after, out, done, raw, raw_scales, wide, loaded, stored):
    def load(k):
        r = pl.ds(pl.multiple_of(k * PART, PART), PART)
        return pltpu.make_async_copy(codes.at[r], raw.at[r], loaded.at[k])

    def store(k):
        r = pl.ds(pl.multiple_of(k * PART, PART), PART)
        return pltpu.make_async_copy(raw.at[r], out.at[r], stored.at[k])

    load_scales = pltpu.make_async_copy(scales, raw_scales, loaded.at[PARTS])
    load_scales.start()
    for k in range(PARTS):
        load(k).start()
    done[...] = jnp.zeros((8, 128), jnp.float32)
    load_scales.wait()
    wide[...] = raw_scales[...].astype(jnp.float32)

    @pl.loop(0, PARTS)
    def _(k):
        load(k).wait()
        rows = wide[pl.ds(pl.multiple_of(k * 8, 8), 8), :]
        for i in range(PART // 16):
            at = pl.ds(pl.multiple_of(k * PART + i * 16, 16), 16)
            s = jnp.broadcast_to(rows[i : i + 1, :], (16, COLS)).astype(jnp.bfloat16)
            raw[at, :] = raw[at, :] * s
        store(k).start()

    for k in range(PARTS):
        store(k).wait()


def decode(codes, scales, after):
    return pl.pallas_call(
        decode_kernel,
        in_specs=[HBM, HBM, ANY],
        out_specs=[HBM, VMEM],
        out_shape=[
            jax.ShapeDtypeStruct((WIDTH, COLS), jnp.bfloat16),
            jax.ShapeDtypeStruct((8, 128), jnp.float32),
        ],
        scratch_shapes=[
            pltpu.VMEM((WIDTH, COLS), jnp.bfloat16),
            pltpu.VMEM((WIDTH // 16, COLS), jnp.bfloat16),
            pltpu.VMEM((WIDTH // 16, COLS), jnp.float32),
            pltpu.SemaphoreType.DMA((PARTS + 1,)),
            pltpu.SemaphoreType.DMA((PARTS,)),
        ],
        compiler_params=DECODE_PARAMS,
        cost_estimate=pl.CostEstimate(flops=WIDTH * COLS, bytes_accessed=14 << 20, transcendentals=0),
        name="decode",
    )(codes, scales, after)


BN = 512
TILES = COLS // BN
HALF = 32
Z_ORDER = (6, 1, 7, 0, 4, 3, 5, 2)


def product_kernel(place, *refs):
    slabs, weight, outs, (rows32, rows16, tiles, sems) = refs[:8], refs[8], refs[9:17], refs[17:]
    copies = [
        pltpu.make_async_copy(weight.at[:, pl.ds(k * BN, BN)], tiles.at[k], sems.at[k])
        for k in range(TILES)
    ]
    for copy in copies:
        copy.start()
    my_z, my_y, my_x, my_c = place[0], place[1], place[2], place[3]
    biggest = jnp.zeros((8, WIDTH), jnp.float32)
    for j, slab in enumerate(slabs):
        z = slab_place(j, my_x, my_c)
        z_step = lax.rem(z - my_z + NZ, NZ)
        z_at = jnp.int32(0)
        for k, step in enumerate(Z_ORDER):
            z_at = jnp.where(z_step == step, k, z_at)
        for y in range(NY):
            y_step = lax.rem(y - my_y + NY, NY)
            piece = slab[y * OWN : (y + 1) * OWN, :]
            biggest = jnp.maximum(biggest, jnp.abs(piece))
            at = pl.multiple_of(y_step * (NZ * OWN) + z_at * OWN, OWN)
            rows32[pl.ds(at, OWN), :] = piece
    rows16[...] = rows32[...].astype(jnp.bfloat16)
    top = jnp.full((8, 128), jnp.max(biggest), jnp.float32)
    for out in outs:
        for k in range(HALF // 8):
            out[k * 8 : (k + 1) * 8, COLS:] = top
    for k, copy in enumerate(copies):
        copy.wait()
        total = jnp.dot(rows16[...], tiles[k], preferred_element_type=jnp.float32)
        for i, out in enumerate(outs):
            out[:, k * BN : (k + 1) * BN] = total[i * HALF : (i + 1) * HALF, :]


def product(slabs, weight, place):
    return pl.pallas_call(
        product_kernel,
        in_specs=[SMEM] + [VMEM] * 8 + [HBM],
        out_specs=[VMEM] * 8,
        out_shape=[jax.ShapeDtypeStruct((HALF, WIDE), jnp.float32)] * 8,
        scratch_shapes=[
            pltpu.VMEM((ROWS, WIDTH), jnp.float32),
            pltpu.VMEM((ROWS, WIDTH), jnp.bfloat16),
            pltpu.VMEM((TILES, WIDTH, BN), jnp.bfloat16),
            pltpu.SemaphoreType.DMA((TILES,)),
        ],
        compiler_params=WEIGHT_PARAMS,
        name="product",
    )(place, *slabs, weight)


def relay_kernel(own, arrived, after, out):
    out[:, :COLS] = own[:, :COLS] + arrived[:, :COLS]
    out[:, COLS:] = jnp.maximum(own[:, COLS:], arrived[:, COLS:])


def relay(own, arrived, after):
    return pl.pallas_call(
        relay_kernel,
        in_specs=[VMEM] * 2 + [ANY],
        out_specs=VMEM,
        out_shape=jax.ShapeDtypeStruct((HALF, WIDE), jnp.float32),
        compiler_params=PARAMS,
        name="relay",
    )(own, arrived, after)


def y_sum_kernel(a, b, c, after, *outs):
    top = jnp.maximum(jnp.maximum(a[:8, COLS:], b[:8, COLS:]), c[:8, COLS:])
    for k, out in enumerate(outs):
        r = slice(k * OWN, (k + 1) * OWN)
        out[:, :COLS] = a[r, :COLS] + b[r, :COLS] + c[r, :COLS]
        out[:, COLS:] = top


def y_sum(a, b, c, after):
    return pl.pallas_call(
        y_sum_kernel,
        in_specs=[VMEM] * 3 + [ANY],
        out_specs=[VMEM] * (HALF // OWN),
        out_shape=[jax.ShapeDtypeStruct((OWN, WIDE), jnp.float32)] * (HALF // OWN),
        compiler_params=PARAMS,
        name="y_sum",
    )(a, b, c, after)


def z_sum_kernel(*refs):
    parts, residual, scale, summed, rounded, squares, top = refs[:NZ], *refs[NZ:]
    total = parts[0][:, :COLS]
    peak = parts[0][:, COLS:]
    for part in parts[1:]:
        total += part[:, :COLS]
        peak = jnp.maximum(peak, part[:, COLS:])
    total = residual[...].astype(jnp.float32) + total * scale[0]
    summed[...] = total
    rounded[...] = total.astype(jnp.bfloat16)
    squares[...] = jnp.broadcast_to(jnp.sum(total * total, axis=1, keepdims=True), (OWN, 128))
    top[...] = peak


def z_sum(parts, residual, weight_scale):
    return pl.pallas_call(
        z_sum_kernel,
        in_specs=[VMEM] * (NZ + 1) + [SMEM],
        out_specs=[VMEM] * 4,
        out_shape=[
            jax.ShapeDtypeStruct((OWN, COLS), jnp.float32),
            jax.ShapeDtypeStruct((OWN, COLS), jnp.bfloat16),
            jax.ShapeDtypeStruct((OWN, 128), jnp.float32),
            jax.ShapeDtypeStruct((OWN, 128), jnp.float32),
        ],
        compiler_params=PARAMS,
        name="z_sum",
    )(*parts, residual, weight_scale)


def norm_kernel(summed, a, b, c, d, gain, after, out):
    mean = (a[...] + b[...] + c[...] + d[...]) * (1.0 / (COLS * N_TENSOR))
    factor = lax.rsqrt(mean + 1e-05)[:, :1]
    out[...] = (summed[...] * factor * gain[...].astype(jnp.float32)).astype(jnp.bfloat16)


def norm(summed, squares, gain, after):
    return pl.pallas_call(
        norm_kernel,
        in_specs=[VMEM] * 6 + [ANY],
        out_specs=VMEM,
        out_shape=jax.ShapeDtypeStruct((OWN, COLS), jnp.bfloat16),
        compiler_params=PARAMS,
        name="norm",
    )(summed, *squares, gain, after)


def split3(value):
    parts = []
    for _ in range(3):
        part = value.astype(jnp.bfloat16)
        parts.append(part)
        value = value - part.astype(jnp.float32)
    return parts


def block_maxima(rows, factor, wide):
    lane = lax.broadcasted_iota(jnp.int32, (SLAB, WIDTH), 1)
    for k, slab in enumerate(rows):
        at = slice(k * SLAB, (k + 1) * SLAB)
        big = jnp.abs(slab[...])
        for shift in (1, 2, 4, 8):
            up = pltpu.roll(big, WIDTH - shift, 1)
            down = pltpu.roll(big, shift, 1)
            big = jnp.maximum(big, jnp.where((lane & shift) == 0, up, down))
        wide[at, :] = big
        factor[at, :] = 6.0 / big
    block = lax.broadcasted_iota(jnp.int32, (WIDTH, WIDTH // 16), 1)
    unit = lax.broadcasted_iota(jnp.int32, (WIDTH, WIDTH // 16), 0)
    first = jnp.where(unit == 16 * block, 1.0, 0.0).astype(jnp.bfloat16)
    return sum(
        jnp.dot(part, first, preferred_element_type=jnp.float32) for part in split3(wide[...])
    )


def mine_kernel(*refs):
    rows, (after, narrow, factor, wide) = refs[:4], refs[4:]
    narrow[...] = block_maxima(rows, factor, wide)


def theirs_kernel(place, *refs):
    rows, (mine, after, narrow, factor, wide, all_rows) = refs[:4], refs[4:]
    maxima = block_maxima(rows, factor, wide)
    for dc, half in enumerate((mine[...], maxima)):
        for dx in range(NX):
            t = slab_place(dc * NX + dx, place[2], place[3])
            at = pl.ds(pl.multiple_of(t * SLAB, SLAB), SLAB)
            all_rows[at, :] = half[dx * SLAB : (dx + 1) * SLAB, :]
    narrow[...] = all_rows[...].T


def mine_blocks(rows, after):
    return pl.pallas_call(
        mine_kernel,
        in_specs=[VMEM] * 4 + [ANY],
        out_specs=[VMEM] * 2,
        out_shape=[
            jax.ShapeDtypeStruct((ROWS // 2, WIDTH // 16), jnp.float32),
            jax.ShapeDtypeStruct((ROWS // 2, WIDTH), jnp.float32),
        ],
        scratch_shapes=[pltpu.VMEM((ROWS // 2, WIDTH), jnp.float32)],
        compiler_params=PARAMS,
        name="mine_blocks",
    )(*rows, after)


def theirs_blocks(place, rows, mine, after):
    return pl.pallas_call(
        theirs_kernel,
        in_specs=[SMEM] + [VMEM] * 5 + [ANY],
        out_specs=[VMEM] * 2,
        out_shape=[
            jax.ShapeDtypeStruct((WIDTH // 16, ROWS), jnp.float32),
            jax.ShapeDtypeStruct((ROWS // 2, WIDTH), jnp.float32),
        ],
        scratch_shapes=[
            pltpu.VMEM((ROWS // 2, WIDTH), jnp.float32),
            pltpu.VMEM((ROWS, WIDTH // 16), jnp.float32),
        ],
        compiler_params=PARAMS,
        name="theirs_blocks",
    )(place, *rows, mine, after)


def encode_kernel(place, *refs):
    slabs, factors, (narrow, peak, payload, block_scales, done) = refs[:8], refs[8:10], refs[10:]
    done[...] = peak[...]
    my_x, my_c = place[2], place[3]
    top = peak[...]
    low = top / 64.0
    most = (6.0 / low)[:1, :1]
    block_scales[...] = jnp.maximum(narrow[...], low[:1, :1]) * (448.0 / top)[:1, :1]
    for j, slab in enumerate(slabs):
        at = pl.ds(pl.multiple_of(slab_place(j, my_x, my_c) * SLAB, SLAB), SLAB)
        k = j % NX * SLAB
        value = slab[...] * jnp.minimum(factors[j // NX][k : k + SLAB, :], most)
        payload[at, :] = value.astype(jnp.bfloat16)


def encode(slabs, factors, place, narrow, peak):
    return pl.pallas_call(
        encode_kernel,
        in_specs=[SMEM] + [VMEM] * 12,
        out_specs=[VMEM] * 3,
        out_shape=[
            jax.ShapeDtypeStruct((ROWS, WIDTH), jnp.bfloat16),
            jax.ShapeDtypeStruct((WIDTH // 16, ROWS), jnp.float32),
            jax.ShapeDtypeStruct((OWN, 128), jnp.float32),
        ],
        compiler_params=PARAMS,
        name="encode",
    )(place, *slabs, *factors, narrow, peak)


def on_device(gate_pre, up_pre, down_codes, down_scales, weight_scale, residual, norm_gain):
    place = jnp.stack([lax.axis_index(a) for a in ("z", "y", "x", "c")]).astype(jnp.int32)
    first_row = (place[2] * NC + place[3]) * SLAB
    gate = lax.dynamic_slice_in_dim(gate_pre, first_row, SLAB, 0).astype(jnp.float32)
    up = lax.dynamic_slice_in_dim(up_pre, first_row, SLAB, 0).astype(jnp.float32)
    inner = inner_transform((gate / (1.0 + jnp.exp(-gate)) * up).astype(jnp.bfloat16))
    one_row = lax.all_to_all(inner, ("z", "y"), 0, 0, tiled=True)
    turned = outer_transform(one_row)
    own = lax.all_to_all(turned, ("z", "y"), 0, 0, tiled=True)

    mine = [moved(own, "x", k) for k in (1, 2, 3)]
    weight, done = decode(down_codes, down_scales, own)
    mine = [hand_on(block, done) for block in [own] + mine]
    theirs = [moved(block, "c", 1) for block in mine]
    slabs = mine + theirs
    here_a, here_b, ahead_a, ahead_b, far_a, far_b, behind_a, behind_b = product(slabs, weight, place)
    first, second = moved(far_a, "y", 1), moved(far_b, "y", -1)
    ahead_b, behind_a = moved(ahead_b, "y", 1), moved(behind_a, "y", -1)
    mine_most, mine_factor = mine_blocks(mine, here_a)
    ahead_a, behind_b = relay(ahead_a, first, mine_most), relay(behind_b, second, mine_most)
    narrow, theirs_factor = theirs_blocks(place, theirs, mine_most, behind_b)
    sums_a = y_sum(here_a, moved(ahead_a, "y", 1), behind_a, narrow)
    sums_b = y_sum(here_b, ahead_b, moved(behind_b, "y", -1), narrow)
    sums = [*sums_a, *sums_b]
    parts = [moved(part, "z", step) if step else part for part, step in zip(sums, Z_ORDER)]
    summed, rounded, squares, peak = z_sum(parts, residual, weight_scale)
    squares = squares + moved(squares, "c", 1)
    others = [moved(squares, "x", 1), moved(squares, "x", 2), moved(squares, "x", 3)]
    payload, block_scales, done = encode(
        slabs, (mine_factor, theirs_factor), place, narrow, peak
    )
    normed = norm(summed, [squares] + others, norm_gain.reshape(1, COLS), done)
    return payload, block_scales.T, rounded, normed


def solution(mesh):
    mesh = Mesh(mesh.devices.reshape(NZ, NY, NX, NC), ("z", "y", "x", "c"))
    pipe, tensor = ("z", "y"), ("x", "c")
    in_specs = (
        P(None, pipe),
        P(None, pipe),
        P(pipe, tensor),
        P(pipe, tensor),
        P(),
        P(pipe, tensor),
        P(tensor),
    )
    out_specs = (P(None, pipe), P(None, pipe), P(pipe, tensor), P(pipe, tensor))
    return jax.shard_map(
        on_device, mesh=mesh, in_specs=in_specs, out_specs=out_specs, check_vma=False
    )
```

```python
import jax
import jax.numpy as jnp
from jax import lax
from jax.experimental import pallas as pl
from jax.experimental.pallas import tpu as pltpu
from jax.sharding import Mesh
from jax.sharding import PartitionSpec as P

NZ, NY, NX, NC = 8, 4, 4, 2
N_PIPE, N_TENSOR = NZ * NY, NX * NC
ROWS, GROUPS, INNER = 256, 13, 128
WIDTH = GROUPS * INNER
COLS = 2048
WIDE = COLS + 128
SLAB = ROWS // N_TENSOR
OWN = ROWS // N_PIPE
SIZES = {"z": NZ, "y": NY, "x": NX, "c": NC}
VMEM = pl.BlockSpec(memory_space=pltpu.VMEM)
SMEM = pl.BlockSpec(memory_space=pltpu.SMEM)
ANY = pl.BlockSpec(memory_space=pl.ANY)
HBM = pl.BlockSpec(memory_space=pltpu.HBM)
PARAMS = pltpu.CompilerParams(vmem_limit_bytes=16 * 1024 * 1024)
DECODE_PARAMS = pltpu.CompilerParams(vmem_limit_bytes=50 * 1024 * 1024)
WEIGHT_PARAMS = pltpu.CompilerParams(vmem_limit_bytes=46 * 1024 * 1024)
def moved(block, axis, step):
    count = SIZES[axis]
    return lax.ppermute(block, axis, [(i, (i + step) % count) for i in range(count)])


def sign_matrix(order, scale):
    i = lax.broadcasted_iota(jnp.int32, (order, order), 0)
    j = lax.broadcasted_iota(jnp.int32, (order, order), 1)
    odd = i & j
    for shift in (4, 2, 1):
        odd = odd ^ (odd >> shift)
    return jnp.where((odd & 1) == 1, -scale, scale).astype(jnp.float32)


def inner_kernel(hidden, out):
    had = sign_matrix(INNER, 1.0 / 64.0).astype(jnp.bfloat16)
    for c in range(GROUPS):
        cols = slice(c * INNER, (c + 1) * INNER)
        out[:, cols] = jnp.dot(hidden[:, cols], had, preferred_element_type=jnp.float32)


def inner_transform(hidden):
    return pl.pallas_call(
        inner_kernel,
        in_specs=[VMEM],
        out_specs=VMEM,
        out_shape=jax.ShapeDtypeStruct((SLAB, WIDTH), jnp.float32),
        compiler_params=PARAMS,
        name="inner_transform",
    )(hidden)


def outer_kernel(block, out):
    out[...] = jnp.dot(
        sign_matrix(N_PIPE, 1.0),
        block[...],
        preferred_element_type=jnp.float32,
        precision=lax.Precision.HIGHEST,
    )


def outer_transform(block):
    return pl.pallas_call(
        outer_kernel,
        in_specs=[VMEM],
        out_specs=VMEM,
        out_shape=jax.ShapeDtypeStruct((N_PIPE, WIDTH), jnp.float32),
        compiler_params=PARAMS,
        name="outer_transform",
    )(block)


def hand_on_kernel(block, after, out):
    out[...] = block[...]


def hand_on(block, after):
    return pl.pallas_call(
        hand_on_kernel,
        in_specs=[VMEM, ANY],
        out_specs=VMEM,
        out_shape=jax.ShapeDtypeStruct(block.shape, block.dtype),
        compiler_params=PARAMS,
        name="hand_on",
    )(block, after)


def slab_place(j, my_x, my_c):
    return lax.rem(my_x + NX - j % NX, NX) * NC + lax.rem(my_c + j // NX, NC)


PART = 128
PARTS = WIDTH // PART


def decode_kernel(codes, scales, after, out, done, raw, raw_scales, wide, loaded, stored):
    def load(k):
        r = pl.ds(pl.multiple_of(k * PART, PART), PART)
        return pltpu.make_async_copy(codes.at[r], raw.at[r], loaded.at[k])

    def store(k):
        r = pl.ds(pl.multiple_of(k * PART, PART), PART)
        return pltpu.make_async_copy(raw.at[r], out.at[r], stored.at[k])

    load_scales = pltpu.make_async_copy(scales, raw_scales, loaded.at[PARTS])
    load_scales.start()
    for k in range(PARTS):
        load(k).start()
    done[...] = jnp.zeros((8, 128), jnp.float32)
    load_scales.wait()
    wide[...] = raw_scales[...].astype(jnp.float32)

    @pl.loop(0, PARTS)
    def _(k):
        load(k).wait()
        rows = wide[pl.ds(pl.multiple_of(k * 8, 8), 8), :]
        for i in range(PART // 16):
            at = pl.ds(pl.multiple_of(k * PART + i * 16, 16), 16)
            s = jnp.broadcast_to(rows[i : i + 1, :], (16, COLS)).astype(jnp.bfloat16)
            raw[at, :] = raw[at, :] * s
        store(k).start()

    for k in range(PARTS):
        store(k).wait()


def decode(codes, scales, after):
    return pl.pallas_call(
        decode_kernel,
        in_specs=[HBM, HBM, ANY],
        out_specs=[HBM, VMEM],
        out_shape=[
            jax.ShapeDtypeStruct((WIDTH, COLS), jnp.bfloat16),
            jax.ShapeDtypeStruct((8, 128), jnp.float32),
        ],
        scratch_shapes=[
            pltpu.VMEM((WIDTH, COLS), jnp.bfloat16),
            pltpu.VMEM((WIDTH // 16, COLS), jnp.bfloat16),
            pltpu.VMEM((WIDTH // 16, COLS), jnp.float32),
            pltpu.SemaphoreType.DMA((PARTS + 1,)),
            pltpu.SemaphoreType.DMA((PARTS,)),
        ],
        compiler_params=DECODE_PARAMS,
        cost_estimate=pl.CostEstimate(flops=WIDTH * COLS, bytes_accessed=14 << 20, transcendentals=0),
        name="decode",
    )(codes, scales, after)


BN = 512
TILES = COLS // BN
HALF = 32
Z_ORDER = (6, 1, 7, 0, 3, 5, 4, 2)


def product_kernel(place, *refs):
    slabs, weight, outs, (rows32, rows16, tiles, sems) = refs[:8], refs[8], refs[9:17], refs[17:]
    copies = [
        pltpu.make_async_copy(weight.at[:, pl.ds(k * BN, BN)], tiles.at[k], sems.at[k])
        for k in range(TILES)
    ]
    for copy in copies:
        copy.start()
    my_z, my_y, my_x, my_c = place[0], place[1], place[2], place[3]
    biggest = jnp.zeros((8, WIDTH), jnp.float32)
    for j, slab in enumerate(slabs):
        z = slab_place(j, my_x, my_c)
        z_step = lax.rem(z - my_z + NZ, NZ)
        z_at = jnp.int32(0)
        for k, step in enumerate(Z_ORDER):
            z_at = jnp.where(z_step == step, k, z_at)
        for y in range(NY):
            y_step = lax.rem(y - my_y + NY, NY)
            piece = slab[y * OWN : (y + 1) * OWN, :]
            biggest = jnp.maximum(biggest, jnp.abs(piece))
            at = pl.multiple_of(y_step * (NZ * OWN) + z_at * OWN, OWN)
            rows32[pl.ds(at, OWN), :] = piece
    rows16[...] = rows32[...].astype(jnp.bfloat16)
    top = jnp.full((8, 128), jnp.max(biggest), jnp.float32)
    for out in outs:
        for k in range(HALF // 8):
            out[k * 8 : (k + 1) * 8, COLS:] = top
    for k, copy in enumerate(copies):
        copy.wait()
        total = jnp.dot(rows16[...], tiles[k], preferred_element_type=jnp.float32)
        for i, out in enumerate(outs):
            out[:, k * BN : (k + 1) * BN] = total[i * HALF : (i + 1) * HALF, :]


def product(slabs, weight, place):
    return pl.pallas_call(
        product_kernel,
        in_specs=[SMEM] + [VMEM] * 8 + [HBM],
        out_specs=[VMEM] * 8,
        out_shape=[jax.ShapeDtypeStruct((HALF, WIDE), jnp.float32)] * 8,
        scratch_shapes=[
            pltpu.VMEM((ROWS, WIDTH), jnp.float32),
            pltpu.VMEM((ROWS, WIDTH), jnp.bfloat16),
            pltpu.VMEM((TILES, WIDTH, BN), jnp.bfloat16),
            pltpu.SemaphoreType.DMA((TILES,)),
        ],
        compiler_params=WEIGHT_PARAMS,
        name="product",
    )(place, *slabs, weight)


def relay_kernel(own, arrived, after, out):
    out[:, :COLS] = own[:, :COLS] + arrived[:, :COLS]
    out[:, COLS:] = jnp.maximum(own[:, COLS:], arrived[:, COLS:])


def relay(own, arrived, after):
    return pl.pallas_call(
        relay_kernel,
        in_specs=[VMEM] * 2 + [ANY],
        out_specs=VMEM,
        out_shape=jax.ShapeDtypeStruct((HALF, WIDE), jnp.float32),
        compiler_params=PARAMS,
        name="relay",
    )(own, arrived, after)


def y_sum_kernel(a, b, c, after, *outs):
    top = jnp.maximum(jnp.maximum(a[:8, COLS:], b[:8, COLS:]), c[:8, COLS:])
    for k, out in enumerate(outs):
        r = slice(k * OWN, (k + 1) * OWN)
        out[:, :COLS] = a[r, :COLS] + b[r, :COLS] + c[r, :COLS]
        out[:, COLS:] = top


def y_sum(a, b, c, after):
    return pl.pallas_call(
        y_sum_kernel,
        in_specs=[VMEM] * 3 + [ANY],
        out_specs=[VMEM] * (HALF // OWN),
        out_shape=[jax.ShapeDtypeStruct((OWN, WIDE), jnp.float32)] * (HALF // OWN),
        compiler_params=PARAMS,
        name="y_sum",
    )(a, b, c, after)


def z_sum_kernel(*refs):
    parts, residual, scale, summed, rounded, squares, top = refs[:NZ], *refs[NZ:]
    total = parts[0][:, :COLS]
    peak = parts[0][:, COLS:]
    for part in parts[1:]:
        total += part[:, :COLS]
        peak = jnp.maximum(peak, part[:, COLS:])
    total = residual[...].astype(jnp.float32) + total * scale[0]
    summed[...] = total
    rounded[...] = total.astype(jnp.bfloat16)
    squares[...] = jnp.broadcast_to(jnp.sum(total * total, axis=1, keepdims=True), (OWN, 128))
    top[...] = peak


def z_sum(parts, residual, weight_scale):
    return pl.pallas_call(
        z_sum_kernel,
        in_specs=[VMEM] * (NZ + 1) + [SMEM],
        out_specs=[VMEM] * 4,
        out_shape=[
            jax.ShapeDtypeStruct((OWN, COLS), jnp.float32),
            jax.ShapeDtypeStruct((OWN, COLS), jnp.bfloat16),
            jax.ShapeDtypeStruct((OWN, 128), jnp.float32),
            jax.ShapeDtypeStruct((OWN, 128), jnp.float32),
        ],
        compiler_params=PARAMS,
        name="z_sum",
    )(*parts, residual, weight_scale)


def norm_kernel(summed, a, b, c, d, gain, after, out):
    mean = (a[...] + b[...] + c[...] + d[...]) * (1.0 / (COLS * N_TENSOR))
    factor = lax.rsqrt(mean + 1e-05)[:, :1]
    out[...] = (summed[...] * factor * gain[...].astype(jnp.float32)).astype(jnp.bfloat16)


def norm(summed, squares, gain, after):
    return pl.pallas_call(
        norm_kernel,
        in_specs=[VMEM] * 6 + [ANY],
        out_specs=VMEM,
        out_shape=jax.ShapeDtypeStruct((OWN, COLS), jnp.bfloat16),
        compiler_params=PARAMS,
        name="norm",
    )(summed, *squares, gain, after)


def split3(value):
    parts = []
    for _ in range(3):
        part = value.astype(jnp.bfloat16)
        parts.append(part)
        value = value - part.astype(jnp.float32)
    return parts


def block_maxima(rows, factor, wide):
    lane = lax.broadcasted_iota(jnp.int32, (SLAB, WIDTH), 1)
    for k, slab in enumerate(rows):
        at = slice(k * SLAB, (k + 1) * SLAB)
        big = jnp.abs(slab[...])
        for shift in (1, 2, 4, 8):
            up = pltpu.roll(big, WIDTH - shift, 1)
            down = pltpu.roll(big, shift, 1)
            big = jnp.maximum(big, jnp.where((lane & shift) == 0, up, down))
        wide[at, :] = big
        factor[at, :] = 6.0 / big
    block = lax.broadcasted_iota(jnp.int32, (WIDTH, WIDTH // 16), 1)
    unit = lax.broadcasted_iota(jnp.int32, (WIDTH, WIDTH // 16), 0)
    first = jnp.where(unit == 16 * block, 1.0, 0.0).astype(jnp.bfloat16)
    return sum(
        jnp.dot(part, first, preferred_element_type=jnp.float32) for part in split3(wide[...])
    )


def mine_kernel(*refs):
    rows, (after, narrow, factor, wide) = refs[:4], refs[4:]
    narrow[...] = block_maxima(rows, factor, wide)


def theirs_kernel(place, *refs):
    rows, (mine, after, narrow, factor, wide, all_rows) = refs[:4], refs[4:]
    maxima = block_maxima(rows, factor, wide)
    for dc, half in enumerate((mine[...], maxima)):
        for dx in range(NX):
            t = slab_place(dc * NX + dx, place[2], place[3])
            at = pl.ds(pl.multiple_of(t * SLAB, SLAB), SLAB)
            all_rows[at, :] = half[dx * SLAB : (dx + 1) * SLAB, :]
    narrow[...] = all_rows[...].T


def mine_blocks(rows, after):
    return pl.pallas_call(
        mine_kernel,
        in_specs=[VMEM] * 4 + [ANY],
        out_specs=[VMEM] * 2,
        out_shape=[
            jax.ShapeDtypeStruct((ROWS // 2, WIDTH // 16), jnp.float32),
            jax.ShapeDtypeStruct((ROWS // 2, WIDTH), jnp.float32),
        ],
        scratch_shapes=[pltpu.VMEM((ROWS // 2, WIDTH), jnp.float32)],
        compiler_params=PARAMS,
        name="mine_blocks",
    )(*rows, after)


def theirs_blocks(place, rows, mine, after):
    return pl.pallas_call(
        theirs_kernel,
        in_specs=[SMEM] + [VMEM] * 5 + [ANY],
        out_specs=[VMEM] * 2,
        out_shape=[
            jax.ShapeDtypeStruct((WIDTH // 16, ROWS), jnp.float32),
            jax.ShapeDtypeStruct((ROWS // 2, WIDTH), jnp.float32),
        ],
        scratch_shapes=[
            pltpu.VMEM((ROWS // 2, WIDTH), jnp.float32),
            pltpu.VMEM((ROWS, WIDTH // 16), jnp.float32),
        ],
        compiler_params=PARAMS,
        name="theirs_blocks",
    )(place, *rows, mine, after)


def encode_kernel(place, *refs):
    slabs, factors, (narrow, peak, payload, block_scales, done) = refs[:8], refs[8:10], refs[10:]
    done[...] = peak[...]
    my_x, my_c = place[2], place[3]
    top = peak[...]
    low = top / 64.0
    most = (6.0 / low)[:1, :1]
    block_scales[...] = jnp.maximum(narrow[...], low[:1, :1]) * (448.0 / top)[:1, :1]
    for j, slab in enumerate(slabs):
        at = pl.ds(pl.multiple_of(slab_place(j, my_x, my_c) * SLAB, SLAB), SLAB)
        k = j % NX * SLAB
        value = slab[...] * jnp.minimum(factors[j // NX][k : k + SLAB, :], most)
        payload[at, :] = value.astype(jnp.bfloat16)


def encode(slabs, factors, place, narrow, peak):
    return pl.pallas_call(
        encode_kernel,
        in_specs=[SMEM] + [VMEM] * 12,
        out_specs=[VMEM] * 3,
        out_shape=[
            jax.ShapeDtypeStruct((ROWS, WIDTH), jnp.bfloat16),
            jax.ShapeDtypeStruct((WIDTH // 16, ROWS), jnp.float32),
            jax.ShapeDtypeStruct((OWN, 128), jnp.float32),
        ],
        compiler_params=PARAMS,
        name="encode",
    )(place, *slabs, *factors, narrow, peak)


def on_device(gate_pre, up_pre, down_codes, down_scales, weight_scale, residual, norm_gain):
    place = jnp.stack([lax.axis_index(a) for a in ("z", "y", "x", "c")]).astype(jnp.int32)
    first_row = (place[2] * NC + place[3]) * SLAB
    gate = lax.dynamic_slice_in_dim(gate_pre, first_row, SLAB, 0).astype(jnp.float32)
    up = lax.dynamic_slice_in_dim(up_pre, first_row, SLAB, 0).astype(jnp.float32)
    inner = inner_transform((gate / (1.0 + jnp.exp(-gate)) * up).astype(jnp.bfloat16))
    one_row = lax.all_to_all(inner, ("z", "y"), 0, 0, tiled=True)
    turned = outer_transform(one_row)
    own = lax.all_to_all(turned, ("z", "y"), 0, 0, tiled=True)

    mine = [moved(own, "x", k) for k in (1, 2, 3)]
    weight, done = decode(down_codes, down_scales, own)
    mine = [hand_on(block, done) for block in [own] + mine]
    theirs = [moved(block, "c", 1) for block in mine]
    slabs = mine + theirs
    here_a, here_b, ahead_a, ahead_b, far_a, far_b, behind_a, behind_b = product(slabs, weight, place)
    first, second = moved(far_a, "y", 1), moved(far_b, "y", -1)
    ahead_b = moved(ahead_b, "y", 1)
    mine_most, mine_factor = mine_blocks(mine, here_a)
    ahead_a, behind_b = relay(ahead_a, first, mine_most), relay(behind_b, second, mine_most)
    narrow, theirs_factor = theirs_blocks(place, theirs, mine_most, behind_b)
    behind_a = moved(hand_on(behind_a, narrow), "y", -1)
    sums_a = y_sum(here_a, moved(ahead_a, "y", 1), behind_a, narrow)
    sums_b = y_sum(here_b, ahead_b, moved(behind_b, "y", -1), narrow)
    sums = [*sums_a, *sums_b]
    parts = [moved(part, "z", step) if step else part for part, step in zip(sums, Z_ORDER)]
    summed, rounded, squares, peak = z_sum(parts, residual, weight_scale)
    squares = squares + moved(squares, "c", 1)
    others = [moved(squares, "x", 1), moved(squares, "x", 2), moved(squares, "x", 3)]
    payload, block_scales, done = encode(
        slabs, (mine_factor, theirs_factor), place, narrow, peak
    )
    normed = norm(summed, [squares] + others, norm_gain.reshape(1, COLS), done)
    return payload, block_scales.T, rounded, normed


def solution(mesh):
    mesh = Mesh(mesh.devices.reshape(NZ, NY, NX, NC), ("z", "y", "x", "c"))
    pipe, tensor = ("z", "y"), ("x", "c")
    in_specs = (
        P(None, pipe),
        P(None, pipe),
        P(pipe, tensor),
        P(pipe, tensor),
        P(),
        P(pipe, tensor),
        P(tensor),
    )
    out_specs = (P(None, pipe), P(None, pipe), P(pipe, tensor), P(pipe, tensor))
    return jax.shard_map(
        on_device, mesh=mesh, in_specs=in_specs, out_specs=out_specs, check_vma=False
    )
```
